512 devices in a mesh: wide: 64 (over x_hi, z, core), narrow: 8 (over y, x_lo).
Axes of the slice: x: 4 (x_hi: 2, x_lo: 2; x = x_hi * 2 + x_lo), y: 4, z: 16, core: 2. Of those that a mesh axis runs over, the one named last changes fastest.
Arguments:
- density: bfloat16 [1024, 24, 128, 128], P('wide', 'narrow'), may hold values from -2 to 2
- block_list: int32 [1024, 24], replicated, may hold values from -1 to 127, as said below
- product_list: int32 [256, 24], replicated, may hold values from -1 to 127, as said below
Outputs:
- square: bfloat16 [256, 24, 128, 128], P('wide', 'narrow')
- cube: bfloat16 [256, 24, 128, 128], P('wide', 'narrow')
The draws below stay inside these ranges and needn't reach their ends.
Inputs may be any that keep to these rules, and one draw needn't show every extreme that they name: `block_list`: within one block row and one index of narrow the live entries are distinct and stand before the empty ones; each such group has at least one live entry, some group has 3 and some exactly one. The global block column of a live entry lies within cyclic distance 16 of the block row: (column - row) mod 1024 is below 16 or at least 1008. `product_list`: within one product row and one index of narrow the live entries are distinct and stand before the empty ones; each such group has at least one live entry, some group has 3 and some exactly one. The global block column of a live entry lies within cyclic distance 16 of the product row's block row, as for block_list.
All inputs are finite; a program needn't handle non-finite values.
Results may differ from the reference program's by a relative error of at most 0.0049.
Values may be sent and summed in bfloat16 or wider, within the bound.
No kernel may reach another device: no remote copies, remote signals or barrier semaphores. Data moves between devices by JAX's collectives and lax.ppermute only.
A program may use at most 64 MiB of HBM per device.

```python
import jax
import jax.numpy as jnp
from jax import lax

BS = 128
ROWS_DEV = 16
KP = 3
KQ = 3
RB = 4
BAND = 16
NB = 1024
NW = 256
N_NARROW = 8


def band_lists(key, row_ids, slot_count):
    row_count = row_ids.shape[0]
    tile_count = row_count * N_NARROW
    candidates = 2 * BAND // N_NARROW
    order_key, count_key, top_key = jax.random.split(key, 3)
    scores = jax.random.randint(order_key, (tile_count, candidates), 0, 1 << 20)
    scores = scores * candidates + jnp.arange(candidates, dtype=jnp.int32)[None, :]
    chosen = jnp.argsort(scores, axis=1, stable=True)[:, :slot_count].astype(jnp.int32)
    counts = jax.random.randint(count_key, (tile_count,), 1, slot_count + 1)
    fullest = jax.random.randint(top_key, (), 0, tile_count)
    tile_ids = jnp.arange(tile_count, dtype=jnp.int32)
    counts = jnp.where(tile_ids == fullest, slot_count, counts)
    counts = jnp.where(tile_ids == (fullest + 1) % tile_count, 1, counts)
    row_of_tile = jnp.repeat(row_ids, N_NARROW)
    device_of_tile = jnp.tile(jnp.arange(N_NARROW, dtype=jnp.int32), row_count)
    first_offset = -BAND + jnp.mod(device_of_tile - row_of_tile + BAND, N_NARROW)
    global_cols = jnp.mod(row_of_tile[:, None] + first_offset[:, None] + N_NARROW * chosen, NB)
    local_cols = global_cols // N_NARROW
    slot_ids = jnp.arange(slot_count, dtype=jnp.int32)
    entries = jnp.where(slot_ids[None, :] < counts[:, None], local_cols, -1)
    return entries.reshape(row_count, N_NARROW * slot_count).astype(jnp.int32)


def draw_block_list(key, part):
    key = jax.random.fold_in(key, 11)
    return band_lists(key, jnp.arange(NB, dtype=jnp.int32), KP)


def draw_product_list(key, part):
    key = jax.random.fold_in(key, 23)
    window_ids = jnp.arange(NW, dtype=jnp.int32)
    row_ids = window_ids // RB * ROWS_DEV + window_ids % RB * (ROWS_DEV // RB)
    return band_lists(key, row_ids.astype(jnp.int32), KQ)


def levels(own_key, dims, shards, low, top_value):
    def one(axis_at, parts):
        draws = jax.random.uniform(jax.random.fold_in(jax.random.fold_in(own_key, 6), axis_at), (parts,), jnp.float32, low / len(shards), top_value / len(shards))
        return jnp.repeat(jnp.exp(draws), dims[axis_at] // parts).reshape((-1,) + (1,) * (len(dims) - axis_at - 1))

    gain = one(*shards[0])
    for cut in shards[1:]:
        gain = gain * one(*cut)
    return gain


def normal_values(rng, shape, width, bound, cuts=(), kind=jnp.bfloat16):
    drawn = jax.random.normal(rng, shape, jnp.float32) * width
    if len(cuts) > 0:
        drawn = levels(rng, shape, cuts, -0.22, 0.18) * drawn
    return jnp.clip(drawn, min=-bound, max=bound).astype(kind)


def setup_inputs(seed: int = 0) -> dict:
    seeds = jax.random.split(jax.random.key(seed), 4)
    density = normal_values(seeds[0], (NB, N_NARROW * KP, BS, BS), 0.13, 2.0, ((0, 64), (1, 8)))
    block_list = draw_block_list(jax.random.fold_in(seeds[3], 71), 0)
    product_list = draw_product_list(jax.random.fold_in(seeds[3], 71), 0)
    return dict(density=density, block_list=block_list, product_list=product_list)


def window_rows():
    window_ids = jnp.arange(NW, dtype=jnp.int32)
    return ((window_ids // RB) * ROWS_DEV + (window_ids % RB) * (ROWS_DEV // RB)).astype(jnp.int32)


def global_columns(lists, capacity):
    entry_device = jnp.arange(N_NARROW * capacity, dtype=jnp.int32) // capacity
    return (jnp.maximum(lists, 0) * N_NARROW + entry_device[None, :]).astype(jnp.int32)


def row_product(left_blocks, left_cols, left_live, target_cols, target_live, kept, kept_cols, kept_live):
    safe_rows = jnp.where(left_live, left_cols, 0).astype(jnp.int32)
    candidate_cols = kept_cols[safe_rows]
    candidate_live = kept_live[safe_rows]
    matches = (candidate_cols[:, None, :] == target_cols[None, :, None]) & candidate_live[:, None, :]
    matches = matches & left_live[:, None, None] & target_live[None, :, None]
    chosen = jnp.argmax(matches, axis=2).astype(jnp.int32)
    present = jnp.any(matches, axis=2)
    right_blocks = kept[safe_rows[:, None], chosen].astype(jnp.float32) * present[:, :, None, None].astype(jnp.float32)
    result_sum = jnp.einsum("eab,eqbc->qac", left_blocks.astype(jnp.float32), right_blocks, precision=lax.Precision.HIGHEST)
    return (result_sum * target_live[:, None, None].astype(jnp.float32)).astype(jnp.bfloat16)


def reference(density, block_list, product_list):
    kept_live = block_list >= 0
    kept = density * kept_live[:, :, None, None].astype(density.dtype)
    kept_cols = global_columns(block_list, KP)
    target_live_all = product_list >= 0
    target_cols_all = global_columns(product_list, KQ)
    rows_of_window = window_rows()

    def square_row(window_id):
        block_row = rows_of_window[window_id]
        return row_product(kept[block_row], kept_cols[block_row], kept_live[block_row], target_cols_all[window_id], target_live_all[window_id], kept, kept_cols, kept_live)

    square = lax.map(square_row, jnp.arange(NW, dtype=jnp.int32))

    def cube_row(window_id):
        return row_product(square[window_id], target_cols_all[window_id], target_live_all[window_id], target_cols_all[window_id], target_live_all[window_id], kept, kept_cols, kept_live)

    cube = lax.map(cube_row, jnp.arange(NW, dtype=jnp.int32))
    return square, cube
```

```python
import functools

import jax
import jax.numpy as jnp
from jax import lax
from jax.experimental import pallas as pl
from jax.experimental.pallas import tpu as pltpu
from jax.sharding import PartitionSpec as P

Y = 4
GROUP = 4
SOURCES = ((0, 0), (0, 1), (-1, 0), (1, 0), (2, 0), (-1, 1), (1, 1), (2, 1))
HALF = len(SOURCES) // 2


def shifted(x, axis, by):
    peers = lax.axis_size(axis)
    return lax.ppermute(x, axis, [(i, (i + by) % peers) for i in range(peers)])


def moved(a, dy, dx):
    pairs = []
    for n in range(2 * Y):
        y, x = divmod(n, 2)
        pairs.append((n, (y + dy) % Y * 2 + (x ^ dx)))
    return lax.ppermute(a, "narrow", pairs)


def gather_rows(own):
    partner = moved(own, 0, 1)
    lower = moved(own, 1, 0)
    upper = moved(own, -1, 0)
    partner_lower = moved(partner, 1, 0)
    partner_upper = moved(partner, -1, 0)
    far = moved(lower, 1, 0)
    partner_far = moved(partner_upper, -1, 0)
    return (own, partner, lower, upper), (far, partner_lower, partner_upper, partner_far)


def list_kernel(rows_dev, slots, window, total_rows, block_ref, product_ref, *rest):
    codes = rest[0:4]
    counts = rest[4:8]
    near, goals, sem = rest[8:11]
    wide_count = lax.axis_size("wide")
    narrow_count = lax.axis_size("narrow")
    wide_at = lax.axis_index("wide")
    narrow_at = lax.axis_index("narrow")
    copies = []
    for part in range(3):
        owner = lax.rem(wide_at + (part - 1 + wide_count), wide_count)
        copies.append(
            pltpu.make_async_copy(
                block_ref.at[pl.ds(owner * rows_dev, rows_dev)],
                near.at[pl.ds(part * rows_dev, rows_dev)],
                sem.at[part],
            )
        )
    copies.append(
        pltpu.make_async_copy(product_ref.at[pl.ds(wide_at * window, window)], goals, sem.at[3])
    )
    for copy in copies:
        copy.start()
    for copy in copies:
        copy.wait()
    step = rows_dev // window
    ext_rows = 3 * rows_dev - step
    capacity = HALF * slots
    left_pad = HALF * window * slots
    right_pad = ext_rows * slots
    pad = left_pad * 256 + right_pad
    y_at = narrow_at // 2
    x_at = lax.rem(narrow_at, 2)
    for which in range(4):
        stage, half = divmod(which, 2)
        code_ref, count_ref = codes[which], counts[which]

        def one_row(g, _, stage=stage, half=half, code_ref=code_ref, count_ref=count_ref):
            base = g * slots * capacity
            for i in range(slots * capacity):
                code_ref[base + i] = pad
            targets = [goals[g, narrow_at * slots + q] for q in range(slots)]
            found = [jnp.int32(0)] * slots
            for j in range(HALF):
                dy, dx = SOURCES[half * HALF + j]
                source = lax.rem(y_at + (dy + Y), Y) * 2 + lax.rem(x_at + dx, 2)
                for s in range(slots):
                    if stage == 0:
                        col = near[rows_dev + g * step, source * slots + s]
                    else:
                        col = goals[g, source * slots + s]
                    live = col >= 0
                    row = lax.rem(
                        col * narrow_count + source - wide_at * rows_dev + (rows_dev + total_rows),
                        total_rows,
                    )
                    row = jnp.where(live, jnp.minimum(row, ext_rows - 1), 0)
                    left = (j * window + g) * slots + s
                    for t in range(slots):
                        right_col = near[row, narrow_at * slots + t]
                        usable = live & (right_col >= 0)
                        code = left * 256 + row * slots + t
                        for q in range(slots):
                            hit = usable & (right_col == targets[q])

                            @pl.when(hit)
                            def _(q=q, code=code, at=found[q]):
                                code_ref[base + q * capacity + at] = code

                            found[q] = found[q] + hit.astype(jnp.int32)
            most = found[0]
            for q in range(1, slots):
                most = jnp.maximum(most, found[q])
            count_ref[g] = (most + (GROUP - 1)) // GROUP
            return 0

        lax.fori_loop(0, window, one_row, 0)


def build_lists(block_list, product_list, rows_dev, slots, window):
    total_rows = block_list.shape[0]
    capacity = HALF * slots
    codes = jax.ShapeDtypeStruct((window * slots * capacity,), jnp.int32)
    counts = jax.ShapeDtypeStruct((window,), jnp.int32)
    outs = pl.pallas_call(
        functools.partial(list_kernel, rows_dev, slots, window, total_rows),
        out_shape=[codes] * 4 + [counts] * 4,
        in_specs=[pl.BlockSpec(memory_space=pl.ANY)] * 2,
        out_specs=[pl.BlockSpec(memory_space=pltpu.SMEM)] * 8,
        scratch_shapes=[
            pltpu.SMEM((3 * rows_dev, block_list.shape[1]), jnp.int32),
            pltpu.SMEM((window, product_list.shape[1]), jnp.int32),
            pltpu.SemaphoreType.DMA((4,)),
        ],
        name="pair_lists",
        cost_estimate=pl.CostEstimate(flops=0, bytes_accessed=3_000_000, transcendentals=0),
    )(block_list, product_list)
    return [(outs[i], outs[4 + i]) for i in range(4)]


def product_kernel(window, slots, ext_rows, first, code_ref, count_ref, *rest):
    lefts = rest[:HALF]
    below, own, above = rest[HALF : HALF + 3]
    rest = rest[HALF + 3 :]
    if not first:
        start_ref, rest = rest[0], rest[1:]
    out_ref, left_buf, right_buf, total, sem = rest
    rows_dev = own.shape[0]
    step = rows_dev // window
    capacity = HALF * slots
    left_pad = HALF * window * slots
    right_pad = ext_rows * slots
    copies = []
    for j in range(HALF):
        copies.append((lefts[j], left_buf.at[pl.ds(j * window, window)]))
    copies.append((below, right_buf.at[pl.ds(0, rows_dev)]))
    copies.append((own, right_buf.at[pl.ds(rows_dev, rows_dev)]))
    tail = ext_rows - 2 * rows_dev
    copies.append((above.at[pl.ds(0, tail)], right_buf.at[pl.ds(2 * rows_dev, tail)]))
    if not first:
        copies.append((start_ref, total))
    copies = [pltpu.make_async_copy(a, b, sem.at[i]) for i, (a, b) in enumerate(copies)]
    for copy in copies:
        copy.start()
    left_buf[HALF * window] = jnp.zeros(left_buf.shape[1:], left_buf.dtype)
    right_buf[ext_rows] = jnp.zeros(right_buf.shape[1:], right_buf.dtype)
    if first:
        total[...] = jnp.zeros_like(total)
    for copy in copies:
        copy.wait()

    def one_row(g, _):
        def one_group(i, _):
            for q in range(slots):
                at = (g * slots + q) * capacity + i * GROUP
                left, right = [], []
                for m in range(GROUP):
                    code = code_ref[at + m]
                    l, r = code // 256, lax.rem(code, 256)
                    left.append(left_buf[l // slots, lax.rem(l, slots)])
                    right.append(right_buf[r // slots, lax.rem(r, slots)])
                total[g, q] += jnp.dot(
                    jnp.concatenate(left, axis=1),
                    jnp.concatenate(right, axis=0),
                    preferred_element_type=jnp.float32,
                )
            return 0

        lax.fori_loop(0, count_ref[g], one_group, 0)
        return 0

    lax.fori_loop(0, window, one_row, 0)
    out_ref[...] = total[...].astype(out_ref.dtype)


def multiply(lists, lefts, rights, start, window, slots, out_type):
    code, count = lists
    block = lefts[0].shape[2:]
    rows_dev = rights[1].shape[0]
    ext_rows = 3 * rows_dev - rows_dev // window
    first = start is None
    anywhere = pl.BlockSpec(memory_space=pl.ANY)
    scalar = pl.BlockSpec(memory_space=pltpu.SMEM)
    extra = () if first else (start,)
    return pl.pallas_call(
        functools.partial(product_kernel, window, slots, ext_rows, first),
        out_shape=jax.ShapeDtypeStruct((window, slots) + block, out_type),
        in_specs=[scalar] * 2 + [anywhere] * (HALF + 3 + len(extra)),
        out_specs=pl.BlockSpec(memory_space=pltpu.VMEM),
        scratch_shapes=[
            pltpu.VMEM((HALF * window + 1, slots) + block, jnp.bfloat16),
            pltpu.VMEM((ext_rows + 1, slots) + block, jnp.bfloat16),
            pltpu.VMEM((window, slots) + block, jnp.float32),
            pltpu.SemaphoreType.DMA((HALF + 4,)),
        ],
        compiler_params=pltpu.CompilerParams(vmem_limit_bytes=24 * 1024 * 1024),
        name="block_products",
        cost_estimate=pl.CostEstimate(
            flops=300_000_000, bytes_accessed=8_000_000, transcendentals=0
        ),
    )(code, count, *lefts, *rights, *extra)


def per_device(density, block_list, product_list):
    rows_dev, slots = density.shape[:2]
    window = product_list.shape[0] // lax.axis_size("wide")
    step = rows_dev // window
    lists = build_lists(block_list, product_list, rows_dev, slots, window)
    local = density.reshape((window, step) + density.shape[1:])[:, 0]
    early, late = gather_rows(local)
    rights = (shifted(density, "wide", 1), density, shifted(density, "wide", -1))
    part = multiply(lists[0], early, rights, None, window, slots, jnp.float32)
    square = multiply(lists[1], late, rights, part, window, slots, jnp.bfloat16)
    early, late = gather_rows(square)
    part = multiply(lists[2], early, rights, None, window, slots, jnp.float32)
    cube = multiply(lists[3], late, rights, part, window, slots, jnp.bfloat16)
    return square, cube


def solution(mesh):
    placed = P("wide", "narrow", None, None)
    return jax.shard_map(
        per_device,
        mesh=mesh,
        in_specs=(placed, P(), P()),
        out_specs=(placed, placed),
        check_vma=False,
    )
```

```python
import functools

import jax
import jax.numpy as jnp
from jax import lax
from jax.experimental import pallas as pl
from jax.experimental.pallas import tpu as pltpu
from jax.sharding import PartitionSpec as P

Y = 4
LANES = 128
SOURCES = ((0, 0), (0, 1), (-1, 0), (1, 0), (2, 0), (-1, 1), (1, 1), (2, 1))
HALF = len(SOURCES) // 2


def shifted(x, axis, by):
    peers = lax.axis_size(axis)
    return lax.ppermute(x, axis, [(i, (i + by) % peers) for i in range(peers)])


def moved(a, dy, dx):
    pairs = []
    for n in range(2 * Y):
        y, x = divmod(n, 2)
        pairs.append((n, (y + dy) % Y * 2 + (x ^ dx)))
    return lax.ppermute(a, "narrow", pairs)


def gather_rows(own, make_tables):
    partner = moved(own, 0, 1)
    lower = moved(own, 1, 0)
    upper = moved(own, -1, 0)
    partner, tables = lax.optimization_barrier((partner, make_tables()))
    partner_lower = moved(partner, 1, 0)
    partner_upper = moved(partner, -1, 0)
    far = moved(lower, 1, 0)
    partner_far = moved(partner_upper, -1, 0)
    return (own, partner, lower, upper), (far, partner_lower, partner_upper, partner_far), tables


def table_kernel(stage, rows_dev, slots, window, total_rows, block_ref, product_ref, *rest):
    tables = rest[0:2]
    near, goals, sem = rest[2:5]
    wide_count = lax.axis_size("wide")
    narrow_count = lax.axis_size("narrow")
    wide_at = lax.axis_index("wide")
    narrow_at = lax.axis_index("narrow")

    def tile(row):
        return pl.ds(pl.multiple_of(row // LANES * LANES, LANES), LANES)

    copies = []
    for part in range(3):
        owner = lax.rem(wide_at + (part - 1 + wide_count), wide_count)
        copies.append((block_ref.at[:, tile(owner * rows_dev)], near.at[part]))
    copies.append((product_ref.at[:, tile(wide_at * window)], goals))
    copies = [pltpu.make_async_copy(a, b, sem.at[i]) for i, (a, b) in enumerate(copies)]
    for copy in copies:
        copy.start()
    for copy in copies:
        copy.wait()
    step = rows_dev // window
    ext_rows = 3 * rows_dev - step
    pad = ext_rows * slots
    y_at = narrow_at // 2
    x_at = lax.rem(narrow_at, 2)
    first_row = wide_at * rows_dev

    def one_row(g, _):
        lane = lax.rem(wide_at * window + g, LANES)
        own_lane = lax.rem(first_row + g * step, LANES)
        targets = [goals[narrow_at * slots + q, lane] for q in range(slots)]
        targets = [jnp.where(t < 0, -2, t) for t in targets]
        for j, (dy, dx) in enumerate(SOURCES):
            source = lax.rem(y_at + (dy + Y), Y) * 2 + lax.rem(x_at + dx, 2)
            half, at = divmod(j, HALF)
            for s in range(slots):
                if stage == 0:
                    col = near[1, source * slots + s, own_lane]
                else:
                    col = goals[source * slots + s, lane]
                row = lax.rem(
                    col * narrow_count + source - first_row + (rows_dev + total_rows), total_rows
                )
                row = jnp.where(col >= 0, jnp.minimum(row, ext_rows - 1), 0)
                part = row // rows_dev
                right_lane = lax.rem(first_row + row + (total_rows - rows_dev), LANES)
                right = [near[part, narrow_at * slots + t, right_lane] for t in range(slots)]
                right = [jnp.where(col >= 0, r, -1) for r in right]
                for q in range(slots):
                    found = jnp.int32(pad)
                    for t in range(slots):
                        found = jnp.where(right[t] == targets[q], row * slots + t, found)
                    tables[half][(g * slots + q) * HALF * slots + at * slots + s] = found
        return 0

    lax.fori_loop(0, window, one_row, 0)


def build_tables(stage, block_list, product_list, rows_dev, slots, window):
    table = jax.ShapeDtypeStruct((window * slots * HALF * slots,), jnp.int32)
    return pl.pallas_call(
        functools.partial(table_kernel, stage, rows_dev, slots, window, block_list.shape[0]),
        out_shape=[table] * 2,
        in_specs=[pl.BlockSpec(memory_space=pl.ANY)] * 2,
        out_specs=[pl.BlockSpec(memory_space=pltpu.SMEM)] * 2,
        scratch_shapes=[
            pltpu.SMEM((3, block_list.shape[1], LANES), jnp.int32),
            pltpu.SMEM((product_list.shape[1], LANES), jnp.int32),
            pltpu.SemaphoreType.DMA((4,)),
        ],
        name="square_tables" if stage == 0 else "cube_tables",
        cost_estimate=pl.CostEstimate(flops=0, bytes_accessed=6_000_000, transcendentals=0),
    )(block_list.T, product_list.T)


def add_products(window, slots, table, lefts, ext, start, out_ref):
    capacity = HALF * slots
    size = out_ref.shape[2]
    pair = 2
    for g in range(window):
        total = [None if start is None else start[g, q] for q in range(slots)]
        for e in range(0, capacity, pair):
            near = range(e, e + pair)
            left = jnp.concatenate([lefts[i // slots][g, i % slots] for i in near], axis=1)
            right = jnp.concatenate(
                [
                    jnp.concatenate(
                        [ext[table[(g * slots + q) * capacity + i]] for i in near], axis=0
                    )
                    for q in range(slots)
                ],
                axis=1,
            )
            term = jnp.dot(left, right, preferred_element_type=jnp.float32)
            for q in range(slots):
                piece = term[:, q * size : (q + 1) * size]
                total[q] = piece if total[q] is None else total[q] + piece
        for q in range(slots):
            out_ref[g, q] = total[q].astype(out_ref.dtype)


def first_kernel(window, slots, table, *rest):
    lefts, (below, own, above, out_ref, ext, sem) = rest[:HALF], rest[HALF:]
    rows = own.shape[0]
    tail = ext.shape[0] - slots - 2 * rows
    copies = [
        (below, ext.at[pl.ds(0, rows)]),
        (own, ext.at[pl.ds(rows, rows)]),
        (above.at[pl.ds(0, tail)], ext.at[pl.ds(2 * rows, tail)]),
    ]
    copies = [pltpu.make_async_copy(a, b, sem.at[i]) for i, (a, b) in enumerate(copies)]
    for copy in copies:
        copy.start()
    for s in range(slots):
        ext[ext.shape[0] - slots + s] = jnp.zeros(ext.shape[1:], ext.dtype)
    for copy in copies:
        copy.wait()
    add_products(window, slots, table, lefts, ext, None, out_ref)


def next_kernel(window, slots, table, *rest):
    lefts, rest = rest[:HALF], rest[HALF:]
    if len(rest) == 3:
        ext, start, out_ref = rest
    else:
        (ext, out_ref), start = rest, None
    add_products(window, slots, table, lefts, ext, start, out_ref)


LOCAL = pl.BlockSpec(memory_space=pltpu.VMEM)
SCALAR = pl.BlockSpec(memory_space=pltpu.SMEM)
PARAMS = pltpu.CompilerParams(vmem_limit_bytes=16 * 1024 * 1024)
COST = pl.CostEstimate(flops=600_000_000, bytes_accessed=6_000_000, transcendentals=0)


def multiply_first(table, lefts, rights, window, slots):
    block = lefts[0].shape[2:]
    rows = rights[0].shape[0]
    ext_blocks = 3 * rows - rows // window + slots
    return pl.pallas_call(
        functools.partial(first_kernel, window, slots),
        out_shape=(
            jax.ShapeDtypeStruct((window, slots) + block, jnp.float32),
            jax.ShapeDtypeStruct((ext_blocks,) + block, jnp.bfloat16),
        ),
        in_specs=[SCALAR] + [LOCAL] * (HALF + 3),
        out_specs=(LOCAL, LOCAL),
        scratch_shapes=[pltpu.SemaphoreType.DMA((3,))],
        compiler_params=PARAMS,
        name="first_products",
        cost_estimate=COST,
    )(table, *lefts, *rights)


def multiply(table, lefts, ext, start, window, slots, out_type):
    block = lefts[0].shape[2:]
    extra = () if start is None else (start,)
    return pl.pallas_call(
        functools.partial(next_kernel, window, slots),
        out_shape=jax.ShapeDtypeStruct((window, slots) + block, out_type),
        in_specs=[SCALAR] + [LOCAL] * (HALF + 1 + len(extra)),
        out_specs=LOCAL,
        compiler_params=PARAMS,
        name="next_products",
        cost_estimate=COST,
    )(table, *lefts, ext, *extra)


def per_device(density, block_list, product_list):
    rows_dev, slots = density.shape[:2]
    window = product_list.shape[0] // lax.axis_size("wide")
    step = rows_dev // window
    local = density.reshape((window, step) + density.shape[1:])[:, 0]
    density, local = lax.optimization_barrier((density, local))
    early, late, tables = gather_rows(
        local, lambda: build_tables(0, block_list, product_list, rows_dev, slots, window)
    )
    blocks = density.reshape((rows_dev * slots,) + density.shape[2:])
    rights = (shifted(blocks, "wide", 1), blocks, shifted(blocks, "wide", -1))
    part, ext = multiply_first(tables[0], early, rights, window, slots)
    square = multiply(tables[1], late, ext, part, window, slots, jnp.bfloat16)
    square, block_list, product_list = lax.optimization_barrier((square, block_list, product_list))
    early, late, tables = gather_rows(
        square, lambda: build_tables(1, block_list, product_list, rows_dev, slots, window)
    )
    part = multiply(tables[0], early, ext, None, window, slots, jnp.float32)
    cube = multiply(tables[1], late, ext, part, window, slots, jnp.bfloat16)
    return square, cube


def solution(mesh):
    placed = P("wide", "narrow", None, None)
    return jax.shard_map(
        per_device,
        mesh=mesh,
        in_specs=(placed, P(), P()),
        out_specs=(placed, placed),
        check_vma=False,
    )
```

```python
import functools

import jax
import jax.numpy as jnp
from jax import lax
from jax.experimental import pallas as pl
from jax.experimental.pallas import tpu as pltpu
from jax.sharding import PartitionSpec as P

Y = 4
LANES = 128
SOURCES = ((0, 0), (0, 1), (-1, 0), (1, 0), (2, 0), (-1, 1), (1, 1), (2, 1))
HALF = len(SOURCES) // 2


def moved(a, dy, dx):
    pairs = []
    for n in range(2 * Y):
        y, x = divmod(n, 2)
        pairs.append((n, (y + dy) % Y * 2 + (x ^ dx)))
    return lax.ppermute(a, "narrow", pairs)


def gather_rows_by_y(own, table):
    partner = moved(own, 0, 1)
    lower = moved(own, 1, 0)
    upper = moved(own, -1, 0)
    partner, table = lax.optimization_barrier((partner, table))
    partner_upper = moved(partner, -1, 0)
    partner_lower = moved(partner, 1, 0)
    far = moved(lower, 1, 0)
    partner_far = moved(partner_upper, -1, 0)
    return (own, partner, lower, upper), (far, partner_lower, partner_upper, partner_far), table


def gather_rows(own):
    partner = moved(own, 0, 1)
    lower = moved(own, 1, 0)
    upper = moved(own, -1, 0)
    far = moved(own, 2, 0)
    partner_lower = moved(lower, 0, 1)
    partner_upper = moved(upper, 0, 1)
    partner_far = moved(partner, 2, 0)
    return (own, partner, lower, upper), (far, partner_lower, partner_upper, partner_far)


def table_kernel(rows_dev, slots, window, block_ref, product_ref, table_ref):
    total_rows = block_ref.shape[1]
    entries = block_ref.shape[0]
    narrow_count = entries // slots
    narrow_at = lax.axis_index("narrow")
    first_row = lax.axis_index("wide") * rows_dev
    first_goal = lax.axis_index("wide") * window
    step = rows_dev // window
    ext_rows = 3 * rows_dev - step
    pad = ext_rows * slots
    row = lax.broadcasted_iota(jnp.int32, (1, total_rows), 1)
    goal = lax.broadcasted_iota(jnp.int32, (1, product_ref.shape[1]), 1)
    entry = lax.broadcasted_iota(jnp.int32, (entries, 1), 0)
    source = jnp.zeros((entries, 1), jnp.int32)
    for n in range(1, narrow_count):
        source += (entry >= n * slots).astype(jnp.int32)
    ext_row = row - first_row + rows_dev
    ext_row = jnp.where(ext_row < 0, ext_row + total_rows, ext_row)
    ext_row = jnp.where(ext_row >= total_rows, ext_row - total_rows, ext_row)
    inside = ext_row < ext_rows
    mine = [pl.ds(narrow_at * slots + t, 1) for t in range(slots)]
    right = [jnp.where(inside, block_ref[mine[t], :], -1) for t in range(slots)]
    table = jnp.full(table_ref.shape, pad, jnp.int32)
    column = lax.broadcasted_iota(jnp.int32, table_ref.shape, 1)

    def pick(values, where):
        return jnp.sum(jnp.where(where, values, 0), axis=1, keepdims=True)

    for g in range(window):
        at_goal = goal == first_goal + g
        names = []
        for q in range(slots):
            target = pick(product_ref[mine[q], :], at_goal)
            target = jnp.where(target < 0, -2, target)
            name = jnp.zeros((1, total_rows), jnp.int32)
            for t in range(slots):
                name = jnp.where(right[t] == target, ext_row * slots + (t - pad), name)
            names.append(name)
        for stage in range(2):
            if stage == 0:
                col = pick(block_ref[...], row == first_row + g * step)
            else:
                col = pick(product_ref[...], at_goal)
            meets = row == jnp.where(col < 0, -1, col * narrow_count + source)
            for q in range(slots):
                found = pick(names[q], meets) + pad
                table = jnp.where(column == 16 * stage + g * slots + q, found, table)
    table_ref[...] = table


def build_table(block_list, product_list, rows_dev, slots, window):
    return pl.pallas_call(
        functools.partial(table_kernel, rows_dev, slots, window),
        out_shape=jax.ShapeDtypeStruct((block_list.shape[1], LANES), jnp.int32),
        in_specs=[LOCAL] * 2,
        out_specs=LOCAL,
        compiler_params=pltpu.CompilerParams(vmem_limit_bytes=4 * 1024 * 1024),
        name="block_table",
        cost_estimate=pl.CostEstimate(flops=0, bytes_accessed=3_000_000, transcendentals=0),
    )(block_list.T, product_list.T)


LOCAL = pl.BlockSpec(memory_space=pltpu.VMEM)
SCALAR = pl.BlockSpec(memory_space=pltpu.SMEM)
PARAMS = pltpu.CompilerParams(vmem_limit_bytes=8 * 1024 * 1024)
COST = pl.CostEstimate(flops=600_000_000, bytes_accessed=6_000_000, transcendentals=0)


def add_products(stage, half, window, slots, table, lefts, ext, start, out_ref):
    capacity = HALF * slots
    size = out_ref.shape[2]
    pair = 2
    narrow_at = lax.axis_index("narrow")
    y_at = narrow_at // 2
    x_at = lax.rem(narrow_at, 2)
    entry = []
    for dy, dx in SOURCES[half * HALF : (half + 1) * HALF]:
        source = lax.rem(y_at + (dy + Y), Y) * 2 + lax.rem(x_at + dx, 2)
        entry += [source * slots + s for s in range(slots)]
    for g in range(window):
        total = [None if start is None else start[g, q] for q in range(slots)]
        for e in range(0, capacity, pair):
            near = range(e, e + pair)
            left = jnp.concatenate([lefts[i // slots][g, i % slots] for i in near], axis=1)
            right = jnp.concatenate(
                [
                    jnp.concatenate(
                        [ext[table[entry[i], 16 * stage + g * slots + q]] for i in near], axis=0
                    )
                    for q in range(slots)
                ],
                axis=1,
            )
            term = jnp.dot(left, right, preferred_element_type=jnp.float32)
            for q in range(slots):
                piece = term[:, q * size : (q + 1) * size]
                total[q] = piece if total[q] is None else total[q] + piece
        for q in range(slots):
            out_ref[g, q] = total[q].astype(out_ref.dtype)


def first_kernel(window, slots, table, *rest):
    lefts, (chip, own, next_chip, out_ref, ext, sem) = rest[:HALF], rest[HALF:]
    rows = own.shape[0]
    tail = ext.shape[0] - slots - 2 * rows
    even = lax.rem(lax.axis_index("wide"), 2) == 0

    def lay_out(below, above):
        copies = [
            (below, ext.at[pl.ds(0, rows)]),
            (own, ext.at[pl.ds(rows, rows)]),
            (above.at[pl.ds(0, tail)], ext.at[pl.ds(2 * rows, tail)]),
        ]
        copies = [pltpu.make_async_copy(a, b, sem.at[i]) for i, (a, b) in enumerate(copies)]
        for copy in copies:
            copy.start()
        for copy in copies:
            copy.wait()

    for s in range(slots):
        ext[ext.shape[0] - slots + s] = jnp.zeros(ext.shape[1:], ext.dtype)
    pl.when(even)(lambda: lay_out(next_chip, chip))
    pl.when(jnp.logical_not(even))(lambda: lay_out(chip, next_chip))
    add_products(0, 0, window, slots, table, lefts, ext, None, out_ref)


def next_kernel(stage, half, window, slots, table, *rest):
    lefts, rest = rest[:HALF], rest[HALF:]
    if len(rest) == 3:
        ext, start, out_ref = rest
    else:
        (ext, out_ref), start = rest, None
    add_products(stage, half, window, slots, table, lefts, ext, start, out_ref)


def multiply_first(table, lefts, rights, window, slots):
    block = lefts[0].shape[2:]
    rows = rights[0].shape[0]
    ext_blocks = 3 * rows - rows // window + slots
    return pl.pallas_call(
        functools.partial(first_kernel, window, slots),
        out_shape=(
            jax.ShapeDtypeStruct((window, slots) + block, jnp.float32),
            jax.ShapeDtypeStruct((ext_blocks,) + block, jnp.bfloat16),
        ),
        in_specs=[SCALAR] + [LOCAL] * (HALF + 3),
        out_specs=(LOCAL, LOCAL),
        scratch_shapes=[pltpu.SemaphoreType.DMA((3,))],
        compiler_params=PARAMS,
        name="first_products",
        cost_estimate=COST,
    )(table, *lefts, *rights)


def multiply(stage, half, table, lefts, ext, start, window, slots, out_type):
    block = lefts[0].shape[2:]
    extra = () if start is None else (start,)
    return pl.pallas_call(
        functools.partial(next_kernel, stage, half, window, slots),
        out_shape=jax.ShapeDtypeStruct((window, slots) + block, out_type),
        in_specs=[SCALAR] + [LOCAL] * (HALF + 1 + len(extra)),
        out_specs=LOCAL,
        compiler_params=PARAMS,
        name="next_products",
        cost_estimate=COST,
    )(table, *lefts, ext, *extra)


def swapped(x, axis, first):
    peers = lax.axis_size(axis)
    pairs = []
    for i in range(first, peers + first, 2):
        a, b = i % peers, (i + 1) % peers
        pairs += [(a, b), (b, a)]
    return lax.ppermute(x, axis, pairs)


def per_device(density, block_list, product_list):
    rows_dev, slots = density.shape[:2]
    window = product_list.shape[0] // lax.axis_size("wide")
    step = rows_dev // window
    table = build_table(block_list, product_list, rows_dev, slots, window)
    blocks = density.reshape((rows_dev * slots,) + density.shape[2:])
    next_chip = swapped(blocks, "wide", 1)
    local = density.reshape((window, step) + density.shape[1:])[:, 0]
    early, late, table = gather_rows_by_y(local, table)
    chip = swapped(blocks, "wide", 0)
    part, ext = multiply_first(table, early, (chip, blocks, next_chip), window, slots)
    square = multiply(0, 1, table, late, ext, part, window, slots, jnp.bfloat16)
    early, late = gather_rows(square)
    part = multiply(1, 0, table, early, ext, None, window, slots, jnp.float32)
    cube = multiply(1, 1, table, late, ext, part, window, slots, jnp.bfloat16)
    return square, cube


def solution(mesh):
    placed = P("wide", "narrow", None, None)
    return jax.shard_map(
        per_device,
        mesh=mesh,
        in_specs=(placed, P(), P()),
        out_specs=(placed, placed),
        check_vma=False,
    )
```

```python
import functools

import jax
import jax.numpy as jnp
from jax import lax
from jax.experimental import pallas as pl
from jax.experimental.pallas import tpu as pltpu
from jax.sharding import PartitionSpec as P

Y = 4
LANES = 128
ORDER_FLOPS = 7_000_000_000
SOURCES = ((0, 0), (0, 1), (-1, 0), (1, 0), (2, 0), (-1, 1), (1, 1), (2, 1))
HALF = len(SOURCES) // 2


def moved(a, dy, dx):
    pairs = []
    for n in range(2 * Y):
        y, x = divmod(n, 2)
        pairs.append((n, (y + dy) % Y * 2 + (x ^ dx)))
    return lax.ppermute(a, "narrow", pairs)


def gather_rows_by_y(own, table):
    partner = moved(own, 0, 1)
    lower = moved(own, 1, 0)
    upper = moved(own, -1, 0)
    partner, table = lax.optimization_barrier((partner, table))
    partner_upper = moved(partner, -1, 0)
    partner_lower = moved(partner, 1, 0)
    far = moved(lower, 1, 0)
    partner_far = moved(partner_upper, -1, 0)
    return (own, partner, lower, upper), (far, partner_lower, partner_upper, partner_far), table


def gather_rows(own):
    partner = moved(own, 0, 1)
    lower = moved(own, 1, 0)
    upper = moved(own, -1, 0)
    far = moved(own, 2, 0)
    partner_lower = moved(lower, 0, 1)
    partner_upper = moved(upper, 0, 1)
    partner_far = moved(partner, 2, 0)
    return (own, partner, lower, upper), (far, partner_lower, partner_upper, partner_far)


def table_kernel(rows_dev, slots, window, block_ref, product_ref, table_ref):
    total_rows = block_ref.shape[1]
    entries = block_ref.shape[0]
    narrow_count = entries // slots
    narrow_at = lax.axis_index("narrow")
    first_row = lax.axis_index("wide") * rows_dev
    first_goal = lax.axis_index("wide") * window
    step = rows_dev // window
    ext_rows = 3 * rows_dev - step
    pad = ext_rows * slots
    row = lax.broadcasted_iota(jnp.int32, (1, total_rows), 1)
    goal = lax.broadcasted_iota(jnp.int32, (1, product_ref.shape[1]), 1)
    entry = lax.broadcasted_iota(jnp.int32, (entries, 1), 0)
    source = jnp.zeros((entries, 1), jnp.int32)
    for n in range(1, narrow_count):
        source += (entry >= n * slots).astype(jnp.int32)
    ext_row = row - first_row + rows_dev
    ext_row = jnp.where(ext_row < 0, ext_row + total_rows, ext_row)
    ext_row = jnp.where(ext_row >= total_rows, ext_row - total_rows, ext_row)
    inside = ext_row < ext_rows
    mine = [pl.ds(narrow_at * slots + t, 1) for t in range(slots)]
    right = [jnp.where(inside, block_ref[mine[t], :], -1) for t in range(slots)]
    table = jnp.full(table_ref.shape, pad, jnp.int32)
    column = lax.broadcasted_iota(jnp.int32, table_ref.shape, 1)

    def pick(values, where):
        return jnp.sum(jnp.where(where, values, 0), axis=1, keepdims=True)

    for g in range(window):
        at_goal = goal == first_goal + g
        names = []
        for q in range(slots):
            target = pick(product_ref[mine[q], :], at_goal)
            target = jnp.where(target < 0, -2, target)
            name = jnp.zeros((1, total_rows), jnp.int32)
            for t in range(slots):
                name = jnp.where(right[t] == target, ext_row * slots + (t - pad), name)
            names.append(name)
        for stage in range(2):
            if stage == 0:
                col = pick(block_ref[...], row == first_row + g * step)
            else:
                col = pick(product_ref[...], at_goal)
            meets = row == jnp.where(col < 0, -1, col * narrow_count + source)
            for q in range(slots):
                found = pick(names[q], meets) + pad
                table = jnp.where(column == 16 * stage + g * slots + q, found, table)
    table_ref[...] = table


def build_table(block_list, product_list, rows_dev, slots, window):
    return pl.pallas_call(
        functools.partial(table_kernel, rows_dev, slots, window),
        out_shape=jax.ShapeDtypeStruct((block_list.shape[1], LANES), jnp.int32),
        in_specs=[LOCAL] * 2,
        out_specs=LOCAL,
        compiler_params=pltpu.CompilerParams(vmem_limit_bytes=4 * 1024 * 1024),
        name="block_table",
        cost_estimate=pl.CostEstimate(flops=0, bytes_accessed=3_000_000, transcendentals=0),
    )(block_list.T, product_list.T)


def passed(table, after):
    def kernel(table_ref, *rest):
        rest[-1][...] = table_ref[...]

    return pl.pallas_call(
        kernel,
        out_shape=jax.ShapeDtypeStruct(table.shape, table.dtype),
        in_specs=[LOCAL] + [pl.BlockSpec(memory_space=pl.ANY)] * len(after),
        out_specs=LOCAL,
        compiler_params=pltpu.CompilerParams(vmem_limit_bytes=1024 * 1024),
        name="pass_table",
        cost_estimate=pl.CostEstimate(flops=ORDER_FLOPS, bytes_accessed=0, transcendentals=0),
    )(table, *after)


LOCAL = pl.BlockSpec(memory_space=pltpu.VMEM)
SCALAR = pl.BlockSpec(memory_space=pltpu.SMEM)
PARAMS = pltpu.CompilerParams(vmem_limit_bytes=8 * 1024 * 1024)
COST = pl.CostEstimate(flops=600_000_000, bytes_accessed=6_000_000, transcendentals=0)


def add_products(stage, sources, window, slots, table, lefts, ext, start, out_ref):
    capacity = len(lefts) * slots
    size = out_ref.shape[2]
    pair = 2
    narrow_at = lax.axis_index("narrow")
    y_at = narrow_at // 2
    x_at = lax.rem(narrow_at, 2)
    entry = []
    for dy, dx in sources:
        source = lax.rem(y_at + (dy + Y), Y) * 2 + lax.rem(x_at + dx, 2)
        entry += [source * slots + s for s in range(slots)]
    for g in range(window):
        total = [None if start is None else start[g, q] for q in range(slots)]
        for e in range(0, capacity, pair):
            near = range(e, e + pair)
            left = jnp.concatenate([lefts[i // slots][g, i % slots] for i in near], axis=1)
            right = jnp.concatenate(
                [
                    jnp.concatenate(
                        [ext[table[entry[i], 16 * stage + g * slots + q]] for i in near], axis=0
                    )
                    for q in range(slots)
                ],
                axis=1,
            )
            term = jnp.dot(left, right, preferred_element_type=jnp.float32)
            for q in range(slots):
                piece = term[:, q * size : (q + 1) * size]
                total[q] = piece if total[q] is None else total[q] + piece
        for q in range(slots):
            out_ref[g, q] = total[q].astype(out_ref.dtype)


def first_kernel(window, slots, table, *rest):
    lefts, (chip, own, next_chip, out_ref, ext, sem) = rest[: 2 * HALF], rest[2 * HALF :]
    rows = own.shape[0]
    tail = ext.shape[0] - slots - 2 * rows
    even = lax.rem(lax.axis_index("wide"), 2) == 0

    def lay_out(below, above):
        copies = [
            (below, ext.at[pl.ds(0, rows)]),
            (own, ext.at[pl.ds(rows, rows)]),
            (above.at[pl.ds(0, tail)], ext.at[pl.ds(2 * rows, tail)]),
        ]
        copies = [pltpu.make_async_copy(a, b, sem.at[i]) for i, (a, b) in enumerate(copies)]
        for copy in copies:
            copy.start()
        for copy in copies:
            copy.wait()

    for s in range(slots):
        ext[ext.shape[0] - slots + s] = jnp.zeros(ext.shape[1:], ext.dtype)
    pl.when(even)(lambda: lay_out(next_chip, chip))
    pl.when(jnp.logical_not(even))(lambda: lay_out(chip, next_chip))
    add_products(0, SOURCES, window, slots, table, lefts, ext, None, out_ref)


def next_kernel(half, window, slots, table, *rest):
    lefts, rest = rest[:HALF], rest[HALF:]
    if len(rest) == 3:
        ext, start, out_ref = rest
    else:
        (ext, out_ref), start = rest, None
    sources = SOURCES[half * HALF : (half + 1) * HALF]
    add_products(1, sources, window, slots, table, lefts, ext, start, out_ref)


def multiply_first(table, lefts, rights, window, slots):
    block = lefts[0].shape[2:]
    rows = rights[0].shape[0]
    ext_blocks = 3 * rows - rows // window + slots
    return pl.pallas_call(
        functools.partial(first_kernel, window, slots),
        out_shape=(
            jax.ShapeDtypeStruct((window, slots) + block, jnp.bfloat16),
            jax.ShapeDtypeStruct((ext_blocks,) + block, jnp.bfloat16),
        ),
        in_specs=[SCALAR] + [LOCAL] * (2 * HALF + 3),
        out_specs=(LOCAL, LOCAL),
        scratch_shapes=[pltpu.SemaphoreType.DMA((3,))],
        compiler_params=PARAMS,
        name="square_products",
        cost_estimate=COST,
    )(table, *lefts, *rights)


def multiply(half, table, lefts, ext, start, window, slots, out_type):
    block = lefts[0].shape[2:]
    extra = () if start is None else (start,)
    return pl.pallas_call(
        functools.partial(next_kernel, half, window, slots),
        out_shape=jax.ShapeDtypeStruct((window, slots) + block, out_type),
        in_specs=[SCALAR] + [LOCAL] * (HALF + 1 + len(extra)),
        out_specs=LOCAL,
        compiler_params=PARAMS,
        name="cube_products",
        cost_estimate=COST,
    )(table, *lefts, ext, *extra)


def swapped(x, axis, first):
    peers = lax.axis_size(axis)
    pairs = []
    for i in range(first, peers + first, 2):
        a, b = i % peers, (i + 1) % peers
        pairs += [(a, b), (b, a)]
    return lax.ppermute(x, axis, pairs)


def per_device(density, block_list, product_list):
    rows_dev, slots = density.shape[:2]
    window = product_list.shape[0] // lax.axis_size("wide")
    step = rows_dev // window
    blocks = density.reshape((rows_dev * slots,) + density.shape[2:])
    next_chip = swapped(blocks, "wide", 1)
    local = density.reshape((window, step) + density.shape[1:])[:, 0]
    table = build_table(block_list, product_list, rows_dev, slots, window)
    early, late, table = gather_rows_by_y(local, table)
    table = passed(table, early[1:] + late)
    chip = swapped(blocks, "wide", 0)
    square, ext = multiply_first(table, early + late, (chip, blocks, next_chip), window, slots)
    early, late = gather_rows(square)
    part = multiply(0, table, early, ext, None, window, slots, jnp.float32)
    cube = multiply(1, table, late, ext, part, window, slots, jnp.bfloat16)
    return square, cube


def solution(mesh):
    placed = P("wide", "narrow", None, None)
    return jax.shard_map(
        per_device,
        mesh=mesh,
        in_specs=(placed, P(), P()),
        out_specs=(placed, placed),
        check_vma=False,
    )
```

```python
import functools

import jax
import jax.numpy as jnp
from jax import lax
from jax.experimental import pallas as pl
from jax.experimental.pallas import tpu as pltpu
from jax.sharding import PartitionSpec as P

Y = 4
LANES = 128
ORDER_FLOPS = 6_000_000_000
SOURCES = ((0, 0), (0, 1), (-1, 0), (1, 0), (2, 0), (-1, 1), (1, 1), (2, 1))


def moved(a, dy, dx):
    pairs = []
    for n in range(2 * Y):
        y, x = divmod(n, 2)
        pairs.append((n, (y + dy) % Y * 2 + (x ^ dx)))
    return lax.ppermute(a, "narrow", pairs)


def gather_rows(own, *beside):
    partner = moved(own, 0, 1)
    upper = moved(own, -1, 0)
    lower = moved(own, 1, 0)
    partner, upper, lower, *beside = lax.optimization_barrier((partner, upper, lower, *beside))
    partner_upper = moved(partner, -1, 0)
    partner_lower = moved(partner, 1, 0)
    far = moved(lower, 1, 0)
    partner_far = moved(partner_upper, -1, 0)
    return (own, partner, lower, upper, far, partner_lower, partner_upper, partner_far), *beside


def table_kernel(rows_dev, slots, window, block_ref, product_ref, table_ref):
    total_rows = block_ref.shape[1]
    entries = block_ref.shape[0]
    narrow_count = entries // slots
    narrow_at = lax.axis_index("narrow")
    first_row = lax.axis_index("wide") * rows_dev
    first_goal = lax.axis_index("wide") * window
    step = rows_dev // window
    ext_rows = 3 * rows_dev - step
    pad = ext_rows * slots
    row = lax.broadcasted_iota(jnp.int32, (1, total_rows), 1)
    goal = lax.broadcasted_iota(jnp.int32, (1, product_ref.shape[1]), 1)
    entry = lax.broadcasted_iota(jnp.int32, (entries, 1), 0)
    source = jnp.zeros((entries, 1), jnp.int32)
    for n in range(1, narrow_count):
        source += (entry >= n * slots).astype(jnp.int32)
    ext_row = row - first_row + rows_dev
    ext_row = jnp.where(ext_row < 0, ext_row + total_rows, ext_row)
    ext_row = jnp.where(ext_row >= total_rows, ext_row - total_rows, ext_row)
    inside = ext_row < ext_rows
    mine = [pl.ds(narrow_at * slots + t, 1) for t in range(slots)]
    right = [jnp.where(inside, block_ref[mine[t], :], -1) for t in range(slots)]
    table = jnp.full(table_ref.shape, pad, jnp.int32)
    column = lax.broadcasted_iota(jnp.int32, table_ref.shape, 1)

    def pick(values, where):
        return jnp.sum(jnp.where(where, values, 0), axis=1, keepdims=True)

    for g in range(window):
        at_goal = goal == first_goal + g
        names = []
        for q in range(slots):
            target = pick(product_ref[mine[q], :], at_goal)
            target = jnp.where(target < 0, -2, target)
            name = jnp.zeros((1, total_rows), jnp.int32)
            for t in range(slots):
                name = jnp.where(right[t] == target, ext_row * slots + (t - pad), name)
            names.append(name)
        for stage in range(2):
            if stage == 0:
                col = pick(block_ref[...], row == first_row + g * step)
            else:
                col = pick(product_ref[...], at_goal)
            meets = row == jnp.where(col < 0, -1, col * narrow_count + source)
            for q in range(slots):
                found = pick(names[q], meets) + pad
                table = jnp.where(column == 16 * stage + g * slots + q, found, table)
    table_ref[...] = table


def build_table(block_list, product_list, rows_dev, slots, window):
    return pl.pallas_call(
        functools.partial(table_kernel, rows_dev, slots, window),
        out_shape=jax.ShapeDtypeStruct((block_list.shape[1], LANES), jnp.int32),
        in_specs=[LOCAL] * 2,
        out_specs=LOCAL,
        compiler_params=pltpu.CompilerParams(vmem_limit_bytes=4 * 1024 * 1024),
        name="block_table",
        cost_estimate=pl.CostEstimate(flops=0, bytes_accessed=3_000_000, transcendentals=0),
    )(block_list.T, product_list.T)


def passed(table, after):
    def kernel(table_ref, *rest):
        rest[-1][...] = table_ref[...]

    return pl.pallas_call(
        kernel,
        out_shape=jax.ShapeDtypeStruct(table.shape, table.dtype),
        in_specs=[LOCAL] + [pl.BlockSpec(memory_space=pl.ANY)] * len(after),
        out_specs=LOCAL,
        compiler_params=pltpu.CompilerParams(vmem_limit_bytes=1024 * 1024),
        name="pass_table",
        cost_estimate=pl.CostEstimate(flops=ORDER_FLOPS, bytes_accessed=0, transcendentals=0),
    )(table, *after)


LOCAL = pl.BlockSpec(memory_space=pltpu.VMEM)
SCALAR = pl.BlockSpec(memory_space=pltpu.SMEM)
PARAMS = pltpu.CompilerParams(vmem_limit_bytes=8 * 1024 * 1024)
COST = pl.CostEstimate(flops=600_000_000, bytes_accessed=6_000_000, transcendentals=0)


def add_products(stage, sources, window, slots, table, lefts, ext, start, out_ref):
    capacity = len(lefts) * slots
    size = out_ref.shape[2]
    pair = 2
    narrow_at = lax.axis_index("narrow")
    y_at = narrow_at // 2
    x_at = lax.rem(narrow_at, 2)
    entry = []
    for dy, dx in sources:
        source = lax.rem(y_at + (dy + Y), Y) * 2 + lax.rem(x_at + dx, 2)
        entry += [source * slots + s for s in range(slots)]
    for g in range(window):
        total = [None if start is None else start[g, q] for q in range(slots)]
        for e in range(0, capacity, pair):
            near = range(e, min(e + pair, capacity))
            left = jnp.concatenate([lefts[i // slots][g, i % slots] for i in near], axis=1)
            right = jnp.concatenate(
                [
                    jnp.concatenate(
                        [ext[table[entry[i], 16 * stage + g * slots + q]] for i in near], axis=0
                    )
                    for q in range(slots)
                ],
                axis=1,
            )
            term = jnp.dot(left, right, preferred_element_type=jnp.float32)
            for q in range(slots):
                piece = term[:, q * size : (q + 1) * size]
                total[q] = piece if total[q] is None else total[q] + piece
        for q in range(slots):
            out_ref[g, q] = total[q].astype(out_ref.dtype)


def first_kernel(window, slots, table, *rest):
    lefts, (chip, own, next_chip, out_ref, ext, sem) = rest[:-6], rest[-6:]
    rows = own.shape[0]
    tail = ext.shape[0] - slots - 2 * rows
    even = lax.rem(lax.axis_index("wide"), 2) == 0

    def lay_out(below, above):
        copies = [
            (below, ext.at[pl.ds(0, rows)]),
            (own, ext.at[pl.ds(rows, rows)]),
            (above.at[pl.ds(0, tail)], ext.at[pl.ds(2 * rows, tail)]),
        ]
        copies = [pltpu.make_async_copy(a, b, sem.at[i]) for i, (a, b) in enumerate(copies)]
        for copy in copies:
            copy.start()
        for copy in copies:
            copy.wait()

    for s in range(slots):
        ext[ext.shape[0] - slots + s] = jnp.zeros(ext.shape[1:], ext.dtype)
    pl.when(even)(lambda: lay_out(next_chip, chip))
    pl.when(jnp.logical_not(even))(lambda: lay_out(chip, next_chip))
    add_products(0, SOURCES, window, slots, table, lefts, ext, None, out_ref)


def next_kernel(sources, window, slots, table, *rest):
    lefts, rest = rest[: len(sources)], rest[len(sources) :]
    if len(rest) == 3:
        ext, start, out_ref = rest
    else:
        (ext, out_ref), start = rest, None
    add_products(1, sources, window, slots, table, lefts, ext, start, out_ref)


def multiply_first(table, lefts, rights, window, slots):
    block = lefts[0].shape[2:]
    rows = rights[0].shape[0]
    ext_blocks = 3 * rows - rows // window + slots
    return pl.pallas_call(
        functools.partial(first_kernel, window, slots),
        out_shape=(
            jax.ShapeDtypeStruct((window, slots) + block, jnp.bfloat16),
            jax.ShapeDtypeStruct((ext_blocks,) + block, jnp.bfloat16),
        ),
        in_specs=[SCALAR] + [LOCAL] * (len(lefts) + 3),
        out_specs=(LOCAL, LOCAL),
        scratch_shapes=[pltpu.SemaphoreType.DMA((3,))],
        compiler_params=PARAMS,
        name="square_products",
        cost_estimate=COST,
    )(table, *lefts, *rights)


def multiply(sources, table, lefts, ext, start, window, slots, out_type):
    block = lefts[0].shape[2:]
    extra = () if start is None else (start,)
    return pl.pallas_call(
        functools.partial(next_kernel, sources, window, slots),
        out_shape=jax.ShapeDtypeStruct((window, slots) + block, out_type),
        in_specs=[SCALAR] + [LOCAL] * (len(lefts) + 1 + len(extra)),
        out_specs=LOCAL,
        compiler_params=PARAMS,
        name="cube_products",
        cost_estimate=COST,
    )(table, *lefts, ext, *extra)


def swapped(x, axis, first):
    peers = lax.axis_size(axis)
    pairs = []
    for i in range(first, peers + first, 2):
        a, b = i % peers, (i + 1) % peers
        pairs += [(a, b), (b, a)]
    return lax.ppermute(x, axis, pairs)


def per_device(density, block_list, product_list):
    rows_dev, slots = density.shape[:2]
    window = product_list.shape[0] // lax.axis_size("wide")
    step = rows_dev // window
    blocks = density.reshape((rows_dev * slots,) + density.shape[2:])
    next_chip = swapped(blocks, "wide", 1)
    local = density.reshape((window, step) + density.shape[1:])[:, 0]
    table = build_table(block_list, product_list, rows_dev, slots, window)
    lefts, table = gather_rows(local, table)
    table = passed(table, lefts[1:])
    chip = swapped(blocks, "wide", 0)
    square, ext = multiply_first(table, lefts, (chip, blocks, next_chip), window, slots)
    (lefts,) = gather_rows(square)
    part = multiply(SOURCES[:-1], table, lefts[:-1], ext, None, window, slots, jnp.float32)
    cube = multiply(SOURCES[-1:], table, lefts[-1:], ext, part, window, slots, jnp.bfloat16)
    return square, cube


def solution(mesh):
    placed = P("wide", "narrow", None, None)
    return jax.shard_map(
        per_device,
        mesh=mesh,
        in_specs=(placed, P(), P()),
        out_specs=(placed, placed),
        check_vma=False,
    )
```

```python
import functools

import jax
import jax.numpy as jnp
from jax import lax
from jax.experimental import pallas as pl
from jax.experimental.pallas import tpu as pltpu
from jax.sharding import PartitionSpec as P

Y = 4
LANES = 128
ORDER_FLOPS = 10_000_000_000
FIRST_FLOPS = 3_000_000_000
SOON_FLOPS = 8000_000_000
HOW = ((False, False), (True, True))
SOON, LATE = (0, 1, 2, 3), (4, 5, 6, 7)
SOURCES = ((0, 0), (0, 1), (-1, 0), (1, 0), (2, 0), (-1, 1), (1, 1), (2, 1))


def moved(a, dy, dx):
    pairs = []
    for n in range(2 * Y):
        y, x = divmod(n, 2)
        pairs.append((n, (y + dy) % Y * 2 + (x ^ dx)))
    return lax.ppermute(a, "narrow", pairs)


def gather_rows(own, table, by_x, direct):
    partner = moved(own, 0, 1)
    lower = moved(own, 1, 0)
    upper = moved(own, -1, 0)
    partner, table = lax.optimization_barrier((partner, table))
    partner_upper = moved(partner, -1, 0)
    partner_lower = moved(lower, 0, 1) if by_x else moved(partner, 1, 0)
    far = moved(lower, 1, 0)
    partner_far = moved(partner, 2, 0) if direct else moved(partner_upper, -1, 0)
    return (own, partner, lower, upper, far, partner_lower, partner_upper, partner_far), table


def table_kernel(rows_dev, slots, window, block_ref, product_ref, table_ref):
    total_rows = block_ref.shape[1]
    entries = block_ref.shape[0]
    narrow_count = entries // slots
    narrow_at = lax.axis_index("narrow")
    first_row = lax.axis_index("wide") * rows_dev
    first_goal = lax.axis_index("wide") * window
    step = rows_dev // window
    ext_rows = 3 * rows_dev - step
    pad = ext_rows * slots
    row = lax.broadcasted_iota(jnp.int32, (1, total_rows), 1)
    goal = lax.broadcasted_iota(jnp.int32, (1, product_ref.shape[1]), 1)
    entry = lax.broadcasted_iota(jnp.int32, (entries, 1), 0)
    source = jnp.zeros((entries, 1), jnp.int32)
    for n in range(1, narrow_count):
        source += (entry >= n * slots).astype(jnp.int32)
    ext_row = row - first_row + rows_dev
    ext_row = jnp.where(ext_row < 0, ext_row + total_rows, ext_row)
    ext_row = jnp.where(ext_row >= total_rows, ext_row - total_rows, ext_row)
    inside = ext_row < ext_rows
    mine = [pl.ds(narrow_at * slots + t, 1) for t in range(slots)]
    right = [jnp.where(inside, block_ref[mine[t], :], -1) for t in range(slots)]
    table = jnp.full(table_ref.shape, pad, jnp.int32)
    column = lax.broadcasted_iota(jnp.int32, table_ref.shape, 1)

    def pick(values, where):
        return jnp.sum(jnp.where(where, values, 0), axis=1, keepdims=True)

    for g in range(window):
        at_goal = goal == first_goal + g
        names = []
        for q in range(slots):
            target = pick(product_ref[mine[q], :], at_goal)
            target = jnp.where(target < 0, -2, target)
            name = jnp.zeros((1, total_rows), jnp.int32)
            for t in range(slots):
                name = jnp.where(right[t] == target, ext_row * slots + (t - pad), name)
            names.append(name)
        for stage in range(2):
            if stage == 0:
                col = pick(block_ref[...], row == first_row + g * step)
            else:
                col = pick(product_ref[...], at_goal)
            meets = row == jnp.where(col < 0, -1, col * narrow_count + source)
            for q in range(slots):
                found = pick(names[q], meets) + pad
                table = jnp.where(column == 16 * stage + g * slots + q, found, table)
    table_ref[...] = table


def build_table(block_list, product_list, rows_dev, slots, window):
    return pl.pallas_call(
        functools.partial(table_kernel, rows_dev, slots, window),
        out_shape=jax.ShapeDtypeStruct((block_list.shape[1], LANES), jnp.int32),
        in_specs=[LOCAL] * 2,
        out_specs=LOCAL,
        compiler_params=pltpu.CompilerParams(vmem_limit_bytes=4 * 1024 * 1024),
        name="block_table",
        cost_estimate=pl.CostEstimate(flops=0, bytes_accessed=3_000_000, transcendentals=0),
    )(block_list.T, product_list.T)


def passed(table, after, flops):
    def kernel(table_ref, *rest):
        rest[-1][...] = table_ref[...]

    return pl.pallas_call(
        kernel,
        out_shape=jax.ShapeDtypeStruct(table.shape, table.dtype),
        in_specs=[LOCAL] + [pl.BlockSpec(memory_space=pl.ANY)] * len(after),
        out_specs=LOCAL,
        compiler_params=pltpu.CompilerParams(vmem_limit_bytes=1024 * 1024),
        name="pass_table",
        cost_estimate=pl.CostEstimate(flops=flops, bytes_accessed=0, transcendentals=0),
    )(table, *after)


LOCAL = pl.BlockSpec(memory_space=pltpu.VMEM)
SCALAR = pl.BlockSpec(memory_space=pltpu.SMEM)
PARAMS = pltpu.CompilerParams(vmem_limit_bytes=8 * 1024 * 1024)
SOON_COST = pl.CostEstimate(flops=SOON_FLOPS, bytes_accessed=6_000_000, transcendentals=0)
COST = pl.CostEstimate(flops=600_000_000, bytes_accessed=6_000_000, transcendentals=0)


def add_products(stage, sources, window, slots, table, lefts, ext, start, out_ref):
    capacity = len(lefts) * slots
    size = out_ref.shape[2]
    pair = 2
    narrow_at = lax.axis_index("narrow")
    y_at = narrow_at // 2
    x_at = lax.rem(narrow_at, 2)
    entry = []
    for dy, dx in sources:
        source = lax.rem(y_at + (dy + Y), Y) * 2 + lax.rem(x_at + dx, 2)
        entry += [source * slots + s for s in range(slots)]
    for g in range(window):
        total = [None if start is None else start[g, q] for q in range(slots)]
        for e in range(0, capacity, pair):
            near = range(e, min(e + pair, capacity))
            left = jnp.concatenate([lefts[i // slots][g, i % slots] for i in near], axis=1)
            right = jnp.concatenate(
                [
                    jnp.concatenate(
                        [ext[table[entry[i], 16 * stage + g * slots + q]] for i in near], axis=0
                    )
                    for q in range(slots)
                ],
                axis=1,
            )
            term = jnp.dot(left, right, preferred_element_type=jnp.float32)
            for q in range(slots):
                piece = term[:, q * size : (q + 1) * size]
                total[q] = piece if total[q] is None else total[q] + piece
        for q in range(slots):
            out_ref[g, q] = total[q].astype(out_ref.dtype)


def first_kernel(window, slots, table, *rest):
    lefts, (chip, own, next_chip, out_ref, ext, sem) = rest[:-6], rest[-6:]
    rows = own.shape[0]
    tail = ext.shape[0] - slots - 2 * rows
    even = lax.rem(lax.axis_index("wide"), 2) == 0

    def lay_out(below, above):
        copies = [
            (below, ext.at[pl.ds(0, rows)]),
            (own, ext.at[pl.ds(rows, rows)]),
            (above.at[pl.ds(0, tail)], ext.at[pl.ds(2 * rows, tail)]),
        ]
        copies = [pltpu.make_async_copy(a, b, sem.at[i]) for i, (a, b) in enumerate(copies)]
        for copy in copies:
            copy.start()
        for copy in copies:
            copy.wait()

    for s in range(slots):
        ext[ext.shape[0] - slots + s] = jnp.zeros(ext.shape[1:], ext.dtype)
    pl.when(even)(lambda: lay_out(next_chip, chip))
    pl.when(jnp.logical_not(even))(lambda: lay_out(chip, next_chip))
    add_products(0, SOURCES, window, slots, table, lefts, ext, None, out_ref)


def next_kernel(sources, window, slots, table, *rest):
    lefts, rest = rest[: len(sources)], rest[len(sources) :]
    if len(rest) == 3:
        ext, start, out_ref = rest
    else:
        (ext, out_ref), start = rest, None
    add_products(1, sources, window, slots, table, lefts, ext, start, out_ref)


def multiply_first(table, lefts, rights, window, slots):
    block = lefts[0].shape[2:]
    rows = rights[0].shape[0]
    ext_blocks = 3 * rows - rows // window + slots
    return pl.pallas_call(
        functools.partial(first_kernel, window, slots),
        out_shape=(
            jax.ShapeDtypeStruct((window, slots) + block, jnp.bfloat16),
            jax.ShapeDtypeStruct((ext_blocks,) + block, jnp.bfloat16),
        ),
        in_specs=[SCALAR] + [LOCAL] * (len(lefts) + 3),
        out_specs=(LOCAL, LOCAL),
        scratch_shapes=[pltpu.SemaphoreType.DMA((3,))],
        compiler_params=PARAMS,
        name="square_products",
        cost_estimate=COST,
    )(table, *lefts, *rights)


def multiply(which, table, lefts, ext, start, window, slots, out_type):
    sources = [SOURCES[j] for j in which]
    lefts = [lefts[j] for j in which]
    block = lefts[0].shape[2:]
    extra = () if start is None else (start,)
    return pl.pallas_call(
        functools.partial(next_kernel, sources, window, slots),
        out_shape=jax.ShapeDtypeStruct((window, slots) + block, out_type),
        in_specs=[SCALAR] + [LOCAL] * (len(lefts) + 1 + len(extra)),
        out_specs=LOCAL,
        compiler_params=PARAMS,
        name="cube_products",
        cost_estimate=SOON_COST if start is None else COST,
    )(table, *lefts, ext, *extra)


def swapped(x, axis, first):
    peers = lax.axis_size(axis)
    pairs = []
    for i in range(first, peers + first, 2):
        a, b = i % peers, (i + 1) % peers
        pairs += [(a, b), (b, a)]
    return lax.ppermute(x, axis, pairs)


def per_device(density, block_list, product_list):
    rows_dev, slots = density.shape[:2]
    window = product_list.shape[0] // lax.axis_size("wide")
    step = rows_dev // window
    blocks = density.reshape((rows_dev * slots,) + density.shape[2:])
    next_chip = swapped(blocks, "wide", 1)
    local = density.reshape((window, step) + density.shape[1:])[:, 0]
    table = build_table(block_list, product_list, rows_dev, slots, window)
    lefts, table = gather_rows(local, table, *HOW[0])
    chip = swapped(blocks, "wide", 0)
    table = passed(table, (lefts[3], lefts[5]), FIRST_FLOPS)
    table = passed(table, lefts[1:], ORDER_FLOPS)
    square, ext = multiply_first(table, lefts, (chip, blocks, next_chip), window, slots)
    lefts, table = gather_rows(square, table, *HOW[1])
    part = multiply(SOON, table, lefts, ext, None, window, slots, jnp.float32)
    cube = multiply(LATE, table, lefts, ext, part, window, slots, jnp.bfloat16)
    return square, cube


def solution(mesh):
    placed = P("wide", "narrow", None, None)
    return jax.shard_map(
        per_device,
        mesh=mesh,
        in_specs=(placed, P(), P()),
        out_specs=(placed, placed),
        check_vma=False,
    )
```

```python
import functools

import jax
import jax.numpy as jnp
from jax import lax
from jax.experimental import pallas as pl
from jax.experimental.pallas import tpu as pltpu
from jax.sharding import PartitionSpec as P

Y = 4
LANES = 128
ORDER_FLOPS = 6_000_000_000
FIRST_FLOPS = 6_000_000_000
SOON_FLOPS = 8000_000_000
HOW = (("", False), ("l", True))
SOON, LATE = (0, 1, 2, 3), (4, 5, 6, 7)
SOURCES = ((0, 0), (0, 1), (-1, 0), (1, 0), (2, 0), (-1, 1), (1, 1), (2, 1))


def moved(a, dy, dx):
    pairs = []
    for n in range(2 * Y):
        y, x = divmod(n, 2)
        pairs.append((n, (y + dy) % Y * 2 + (x ^ dx)))
    return lax.ppermute(a, "narrow", pairs)


def gather_rows(own, table, by_x, direct):
    partner = moved(own, 0, 1)
    lower = moved(own, 1, 0)
    upper = moved(own, -1, 0)
    partner, table = lax.optimization_barrier((partner, table))
    partner_upper = moved(upper, 0, 1) if "u" in by_x else moved(partner, -1, 0)
    partner_lower = moved(lower, 0, 1) if "l" in by_x else moved(partner, 1, 0)
    far = moved(lower, 1, 0)
    if "f" in by_x:
        partner_far = moved(far, 0, 1)
    else:
        partner_far = moved(partner, 2, 0) if direct else moved(partner_upper, -1, 0)
    return (own, partner, lower, upper, far, partner_lower, partner_upper, partner_far), table


def table_kernel(rows_dev, slots, window, block_ref, product_ref, table_ref):
    total_rows = block_ref.shape[1]
    entries = block_ref.shape[0]
    narrow_count = entries // slots
    narrow_at = lax.axis_index("narrow")
    first_row = lax.axis_index("wide") * rows_dev
    first_goal = lax.axis_index("wide") * window
    step = rows_dev // window
    ext_rows = 3 * rows_dev - step
    pad = ext_rows * slots
    row = lax.broadcasted_iota(jnp.int32, (1, total_rows), 1)
    goal = lax.broadcasted_iota(jnp.int32, (1, product_ref.shape[1]), 1)
    entry = lax.broadcasted_iota(jnp.int32, (entries, 1), 0)
    source = jnp.zeros((entries, 1), jnp.int32)
    for n in range(1, narrow_count):
        source += (entry >= n * slots).astype(jnp.int32)
    ext_row = row - first_row + rows_dev
    ext_row = jnp.where(ext_row < 0, ext_row + total_rows, ext_row)
    ext_row = jnp.where(ext_row >= total_rows, ext_row - total_rows, ext_row)
    inside = ext_row < ext_rows
    mine = [pl.ds(narrow_at * slots + t, 1) for t in range(slots)]
    right = [jnp.where(inside, block_ref[mine[t], :], -1) for t in range(slots)]
    table = jnp.full(table_ref.shape, pad, jnp.int32)
    column = lax.broadcasted_iota(jnp.int32, table_ref.shape, 1)

    def pick(values, where):
        return jnp.sum(jnp.where(where, values, 0), axis=1, keepdims=True)

    for g in range(window):
        at_goal = goal == first_goal + g
        names = []
        for q in range(slots):
            target = pick(product_ref[mine[q], :], at_goal)
            target = jnp.where(target < 0, -2, target)
            name = jnp.zeros((1, total_rows), jnp.int32)
            for t in range(slots):
                name = jnp.where(right[t] == target, ext_row * slots + (t - pad), name)
            names.append(name)
        for stage in range(2):
            if stage == 0:
                col = pick(block_ref[...], row == first_row + g * step)
            else:
                col = pick(product_ref[...], at_goal)
            meets = row == jnp.where(col < 0, -1, col * narrow_count + source)
            for q in range(slots):
                found = pick(names[q], meets) + pad
                table = jnp.where(column == 16 * stage + g * slots + q, found, table)
    table_ref[...] = table


def build_table(block_list, product_list, rows_dev, slots, window):
    return pl.pallas_call(
        functools.partial(table_kernel, rows_dev, slots, window),
        out_shape=jax.ShapeDtypeStruct((block_list.shape[1], LANES), jnp.int32),
        in_specs=[LOCAL] * 2,
        out_specs=LOCAL,
        compiler_params=pltpu.CompilerParams(vmem_limit_bytes=4 * 1024 * 1024),
        name="block_table",
        cost_estimate=pl.CostEstimate(flops=0, bytes_accessed=3_000_000, transcendentals=0),
    )(block_list.T, product_list.T)


def passed(table, after, flops):
    def kernel(table_ref, *rest):
        rest[-1][...] = table_ref[...]

    return pl.pallas_call(
        kernel,
        out_shape=jax.ShapeDtypeStruct(table.shape, table.dtype),
        in_specs=[LOCAL] + [pl.BlockSpec(memory_space=pl.ANY)] * len(after),
        out_specs=LOCAL,
        compiler_params=pltpu.CompilerParams(vmem_limit_bytes=1024 * 1024),
        name="pass_table",
        cost_estimate=pl.CostEstimate(flops=flops, bytes_accessed=0, transcendentals=0),
    )(table, *after)


LOCAL = pl.BlockSpec(memory_space=pltpu.VMEM)
SCALAR = pl.BlockSpec(memory_space=pltpu.SMEM)
PARAMS = pltpu.CompilerParams(vmem_limit_bytes=8 * 1024 * 1024)
SOON_COST = pl.CostEstimate(flops=SOON_FLOPS, bytes_accessed=6_000_000, transcendentals=0)
COST = pl.CostEstimate(flops=600_000_000, bytes_accessed=6_000_000, transcendentals=0)


def add_products(stage, sources, window, slots, table, lefts, ext, start, out_ref):
    capacity = len(lefts) * slots
    size = out_ref.shape[2]
    pair = 2
    narrow_at = lax.axis_index("narrow")
    y_at = narrow_at // 2
    x_at = lax.rem(narrow_at, 2)
    entry = []
    for dy, dx in sources:
        source = lax.rem(y_at + (dy + Y), Y) * 2 + lax.rem(x_at + dx, 2)
        entry += [source * slots + s for s in range(slots)]
    for g in range(window):
        total = [None if start is None else start[g, q] for q in range(slots)]
        for e in range(0, capacity, pair):
            near = range(e, min(e + pair, capacity))
            left = jnp.concatenate([lefts[i // slots][g, i % slots] for i in near], axis=1)
            right = jnp.concatenate(
                [
                    jnp.concatenate(
                        [ext[table[entry[i], 16 * stage + g * slots + q]] for i in near], axis=0
                    )
                    for q in range(slots)
                ],
                axis=1,
            )
            term = jnp.dot(left, right, preferred_element_type=jnp.float32)
            for q in range(slots):
                piece = term[:, q * size : (q + 1) * size]
                total[q] = piece if total[q] is None else total[q] + piece
        for q in range(slots):
            out_ref[g, q] = total[q].astype(out_ref.dtype)


def first_kernel(window, slots, table, *rest):
    lefts, (next_chip, own, chip, out_ref, ext, sem) = rest[:-6], rest[-6:]
    rows = own.shape[0]
    tail = ext.shape[0] - slots - 2 * rows
    even = lax.rem(lax.axis_index("wide"), 2) == 0

    def lay_out(below, above):
        copies = [
            (below, ext.at[pl.ds(0, rows)]),
            (own, ext.at[pl.ds(rows, rows)]),
            (above.at[pl.ds(0, tail)], ext.at[pl.ds(2 * rows, tail)]),
        ]
        copies = [pltpu.make_async_copy(a, b, sem.at[i]) for i, (a, b) in enumerate(copies)]
        for copy in copies:
            copy.start()
        for copy in copies:
            copy.wait()

    for s in range(slots):
        ext[ext.shape[0] - slots + s] = jnp.zeros(ext.shape[1:], ext.dtype)
    pl.when(even)(lambda: lay_out(next_chip, chip))
    pl.when(jnp.logical_not(even))(lambda: lay_out(chip, next_chip))
    add_products(0, SOURCES, window, slots, table, lefts, ext, None, out_ref)


def next_kernel(sources, window, slots, table, *rest):
    lefts, rest = rest[: len(sources)], rest[len(sources) :]
    if len(rest) == 3:
        ext, start, out_ref = rest
    else:
        (ext, out_ref), start = rest, None
    add_products(1, sources, window, slots, table, lefts, ext, start, out_ref)


def multiply_first(table, lefts, rights, window, slots):
    block = lefts[0].shape[2:]
    rows = rights[0].shape[0]
    ext_blocks = 3 * rows - rows // window + slots
    return pl.pallas_call(
        functools.partial(first_kernel, window, slots),
        out_shape=(
            jax.ShapeDtypeStruct((window, slots) + block, jnp.bfloat16),
            jax.ShapeDtypeStruct((ext_blocks,) + block, jnp.bfloat16),
        ),
        in_specs=[SCALAR] + [LOCAL] * (len(lefts) + 3),
        out_specs=(LOCAL, LOCAL),
        scratch_shapes=[pltpu.SemaphoreType.DMA((3,))],
        compiler_params=PARAMS,
        name="square_products",
        cost_estimate=COST,
    )(table, *lefts, *rights)


def multiply(which, table, lefts, ext, start, window, slots, out_type):
    sources = [SOURCES[j] for j in which]
    lefts = [lefts[j] for j in which]
    block = lefts[0].shape[2:]
    extra = () if start is None else (start,)
    return pl.pallas_call(
        functools.partial(next_kernel, sources, window, slots),
        out_shape=jax.ShapeDtypeStruct((window, slots) + block, out_type),
        in_specs=[SCALAR] + [LOCAL] * (len(lefts) + 1 + len(extra)),
        out_specs=LOCAL,
        compiler_params=PARAMS,
        name="cube_products",
        cost_estimate=SOON_COST if start is None else COST,
    )(table, *lefts, ext, *extra)


def swapped(x, axis, first):
    peers = lax.axis_size(axis)
    pairs = []
    for i in range(first, peers + first, 2):
        a, b = i % peers, (i + 1) % peers
        pairs += [(a, b), (b, a)]
    return lax.ppermute(x, axis, pairs)


def per_device(density, block_list, product_list):
    rows_dev, slots = density.shape[:2]
    window = product_list.shape[0] // lax.axis_size("wide")
    step = rows_dev // window
    blocks = density.reshape((rows_dev * slots,) + density.shape[2:])
    chip = swapped(blocks, "wide", 0)
    next_chip = swapped(blocks, "wide", 1)
    local = density.reshape((window, step) + density.shape[1:])[:, 0]
    table = build_table(block_list, product_list, rows_dev, slots, window)
    lefts, _ = gather_rows(local, (), *HOW[0])
    table = passed(table, (lefts[3], lefts[4], lefts[5]), FIRST_FLOPS)
    table = passed(table, lefts[1:], ORDER_FLOPS)
    square, ext = multiply_first(table, lefts, (next_chip, blocks, chip), window, slots)
    lefts, table = gather_rows(square, table, *HOW[1])
    part = multiply(SOON, table, lefts, ext, None, window, slots, jnp.float32)
    cube = multiply(LATE, table, lefts, ext, part, window, slots, jnp.bfloat16)
    return square, cube


def solution(mesh):
    placed = P("wide", "narrow", None, None)
    return jax.shard_map(
        per_device,
        mesh=mesh,
        in_specs=(placed, P(), P()),
        out_specs=(placed, placed),
        check_vma=False,
    )
```

```python
import functools

import jax
import jax.numpy as jnp
from jax import lax
from jax.experimental import pallas as pl
from jax.experimental.pallas import tpu as pltpu
from jax.sharding import PartitionSpec as P

Y = 4
LANES = 128
ORDER_FLOPS = 6_000_000_000
FIRST_FLOPS = 6_000_000_000
SOON_FLOPS = 8000_000_000
HOW = (("", False), ("l", True))
SOON, LATE = (0, 1, 2, 3), (4, 5, 6, 7)
SOURCES = ((0, 0), (0, 1), (-1, 0), (1, 0), (2, 0), (-1, 1), (1, 1), (2, 1))


def moved(a, dy, dx):
    pairs = []
    for n in range(2 * Y):
        y, x = divmod(n, 2)
        pairs.append((n, (y + dy) % Y * 2 + (x ^ dx)))
    return lax.ppermute(a, "narrow", pairs)


def gather_rows(own, table, by_x, direct):
    partner = moved(own, 0, 1)
    lower = moved(own, 1, 0)
    upper = moved(own, -1, 0)
    partner, table = lax.optimization_barrier((partner, table))
    partner_upper = moved(upper, 0, 1) if "u" in by_x else moved(partner, -1, 0)
    partner_lower = moved(lower, 0, 1) if "l" in by_x else moved(partner, 1, 0)
    far = moved(lower, 1, 0)
    if "f" in by_x:
        partner_far = moved(far, 0, 1)
    else:
        partner_far = moved(partner, 2, 0) if direct else moved(partner_upper, -1, 0)
    return (own, partner, lower, upper, far, partner_lower, partner_upper, partner_far), table


def table_kernel(rows_dev, slots, window, block_ref, product_ref, table_ref):
    total_rows = block_ref.shape[1]
    entries = block_ref.shape[0]
    narrow_count = entries // slots
    narrow_at = lax.axis_index("narrow")
    first_row = lax.axis_index("wide") * rows_dev
    first_goal = lax.axis_index("wide") * window
    step = rows_dev // window
    ext_rows = 3 * rows_dev - step
    pad = ext_rows * slots
    row = lax.broadcasted_iota(jnp.int32, (1, total_rows), 1)
    goal = lax.broadcasted_iota(jnp.int32, (1, product_ref.shape[1]), 1)
    entry = lax.broadcasted_iota(jnp.int32, (entries, 1), 0)
    source = jnp.zeros((entries, 1), jnp.int32)
    for n in range(1, narrow_count):
        source += (entry >= n * slots).astype(jnp.int32)
    ext_row = row - first_row + rows_dev
    ext_row = jnp.where(ext_row < 0, ext_row + total_rows, ext_row)
    ext_row = jnp.where(ext_row >= total_rows, ext_row - total_rows, ext_row)
    inside = ext_row < ext_rows
    mine = [pl.ds(narrow_at * slots + t, 1) for t in range(slots)]
    right = [jnp.where(inside, block_ref[mine[t], :], -1) for t in range(slots)]
    table = jnp.full(table_ref.shape, pad, jnp.int32)
    column = lax.broadcasted_iota(jnp.int32, table_ref.shape, 1)

    def pick(values, where):
        return jnp.sum(jnp.where(where, values, 0), axis=1, keepdims=True)

    for g in range(window):
        at_goal = goal == first_goal + g
        names = []
        for q in range(slots):
            target = pick(product_ref[mine[q], :], at_goal)
            target = jnp.where(target < 0, -2, target)
            name = jnp.zeros((1, total_rows), jnp.int32)
            for t in range(slots):
                name = jnp.where(right[t] == target, ext_row * slots + (t - pad), name)
            names.append(name)
        for stage in range(2):
            if stage == 0:
                col = pick(block_ref[...], row == first_row + g * step)
            else:
                col = pick(product_ref[...], at_goal)
            meets = row == jnp.where(col < 0, -1, col * narrow_count + source)
            for q in range(slots):
                found = pick(names[q], meets) + pad
                table = jnp.where(column == 16 * stage + g * slots + q, found, table)
    table_ref[...] = table


def build_table(block_list, product_list, rows_dev, slots, window):
    return pl.pallas_call(
        functools.partial(table_kernel, rows_dev, slots, window),
        out_shape=jax.ShapeDtypeStruct((block_list.shape[1], LANES), jnp.int32),
        in_specs=[LOCAL] * 2,
        out_specs=LOCAL,
        compiler_params=pltpu.CompilerParams(vmem_limit_bytes=4 * 1024 * 1024),
        name="block_table",
        cost_estimate=pl.CostEstimate(flops=0, bytes_accessed=3_000_000, transcendentals=0),
    )(block_list.T, product_list.T)


def passed(table, after, flops):
    def kernel(table_ref, *rest):
        rest[-1][...] = table_ref[...]

    return pl.pallas_call(
        kernel,
        out_shape=jax.ShapeDtypeStruct(table.shape, table.dtype),
        in_specs=[LOCAL] + [pl.BlockSpec(memory_space=pl.ANY)] * len(after),
        out_specs=LOCAL,
        compiler_params=pltpu.CompilerParams(vmem_limit_bytes=1024 * 1024),
        name="pass_table",
        cost_estimate=pl.CostEstimate(flops=flops, bytes_accessed=0, transcendentals=0),
    )(table, *after)


LOCAL = pl.BlockSpec(memory_space=pltpu.VMEM)
SCALAR = pl.BlockSpec(memory_space=pltpu.SMEM)
PARAMS = pltpu.CompilerParams(vmem_limit_bytes=8 * 1024 * 1024)
SOON_COST = pl.CostEstimate(flops=SOON_FLOPS, bytes_accessed=6_000_000, transcendentals=0)
COST = pl.CostEstimate(flops=600_000_000, bytes_accessed=6_000_000, transcendentals=0)


def add_products(stage, sources, window, slots, table, lefts, ext, start, out_ref, before=None):
    capacity = len(lefts) * slots
    size = out_ref.shape[2]
    pair = 2
    narrow_at = lax.axis_index("narrow")
    y_at = narrow_at // 2
    x_at = lax.rem(narrow_at, 2)
    entry = []
    for dy, dx in sources:
        source = lax.rem(y_at + (dy + Y), Y) * 2 + lax.rem(x_at + dx, 2)
        entry += [source * slots + s for s in range(slots)]
    for g in range(window):
        if g == 1 and before is not None:
            before()
        total = [None if start is None else start[g, q] for q in range(slots)]
        for e in range(0, capacity, pair):
            near = range(e, min(e + pair, capacity))
            left = jnp.concatenate([lefts[i // slots][g, i % slots] for i in near], axis=1)
            right = jnp.concatenate(
                [
                    jnp.concatenate(
                        [ext[table[entry[i], 16 * stage + g * slots + q]] for i in near], axis=0
                    )
                    for q in range(slots)
                ],
                axis=1,
            )
            term = jnp.dot(left, right, preferred_element_type=jnp.float32)
            for q in range(slots):
                piece = term[:, q * size : (q + 1) * size]
                total[q] = piece if total[q] is None else total[q] + piece
        for q in range(slots):
            out_ref[g, q] = total[q].astype(out_ref.dtype)


def first_kernel(window, slots, table, *rest):
    lefts, (next_chip, own, chip, out_ref, ext, sem) = rest[:-6], rest[-6:]
    rows = own.shape[0]
    tail = ext.shape[0] - slots - 2 * rows
    even = lax.rem(lax.axis_index("wide"), 2) == 0

    def lay_out(below, above):
        copies = [
            (below, ext.at[pl.ds(0, rows)]),
            (own, ext.at[pl.ds(rows, rows)]),
            (above.at[pl.ds(0, tail)], ext.at[pl.ds(2 * rows, tail)]),
        ]
        copies = [pltpu.make_async_copy(a, b, sem.at[i]) for i, (a, b) in enumerate(copies)]
        for copy in copies:
            copy.start()
        for copy in copies[:2]:
            copy.wait()

    def wait_above():
        pltpu.make_async_copy(
            chip.at[pl.ds(0, tail)], ext.at[pl.ds(2 * rows, tail)], sem.at[2]
        ).wait()

    for s in range(slots):
        ext[ext.shape[0] - slots + s] = jnp.zeros(ext.shape[1:], ext.dtype)
    pl.when(even)(lambda: lay_out(next_chip, chip))
    pl.when(jnp.logical_not(even))(lambda: lay_out(chip, next_chip))
    add_products(0, SOURCES, window, slots, table, lefts, ext, None, out_ref, wait_above)


def next_kernel(sources, window, slots, table, *rest):
    lefts, rest = rest[: len(sources)], rest[len(sources) :]
    if len(rest) == 3:
        ext, start, out_ref = rest
    else:
        (ext, out_ref), start = rest, None
    add_products(1, sources, window, slots, table, lefts, ext, start, out_ref)


def multiply_first(table, lefts, rights, window, slots):
    block = lefts[0].shape[2:]
    rows = rights[0].shape[0]
    ext_blocks = 3 * rows - rows // window + slots
    return pl.pallas_call(
        functools.partial(first_kernel, window, slots),
        out_shape=(
            jax.ShapeDtypeStruct((window, slots) + block, jnp.bfloat16),
            jax.ShapeDtypeStruct((ext_blocks,) + block, jnp.bfloat16),
        ),
        in_specs=[SCALAR] + [LOCAL] * (len(lefts) + 3),
        out_specs=(LOCAL, LOCAL),
        scratch_shapes=[pltpu.SemaphoreType.DMA((3,))],
        compiler_params=PARAMS,
        name="square_products",
        cost_estimate=COST,
    )(table, *lefts, *rights)


def multiply(which, table, lefts, ext, start, window, slots, out_type):
    sources = [SOURCES[j] for j in which]
    lefts = [lefts[j] for j in which]
    block = lefts[0].shape[2:]
    extra = () if start is None else (start,)
    return pl.pallas_call(
        functools.partial(next_kernel, sources, window, slots),
        out_shape=jax.ShapeDtypeStruct((window, slots) + block, out_type),
        in_specs=[SCALAR] + [LOCAL] * (len(lefts) + 1 + len(extra)),
        out_specs=LOCAL,
        compiler_params=PARAMS,
        name="cube_products",
        cost_estimate=SOON_COST if start is None else COST,
    )(table, *lefts, ext, *extra)


def swapped(x, axis, first):
    peers = lax.axis_size(axis)
    pairs = []
    for i in range(first, peers + first, 2):
        a, b = i % peers, (i + 1) % peers
        pairs += [(a, b), (b, a)]
    return lax.ppermute(x, axis, pairs)


def per_device(density, block_list, product_list):
    rows_dev, slots = density.shape[:2]
    window = product_list.shape[0] // lax.axis_size("wide")
    step = rows_dev // window
    blocks = density.reshape((rows_dev * slots,) + density.shape[2:])
    chip = swapped(blocks, "wide", 0)
    next_chip = swapped(blocks, "wide", 1)
    local = density.reshape((window, step) + density.shape[1:])[:, 0]
    table = build_table(block_list, product_list, rows_dev, slots, window)
    lefts, _ = gather_rows(local, (), *HOW[0])
    table = passed(table, (lefts[3], lefts[4], lefts[5]), FIRST_FLOPS)
    table = passed(table, lefts[1:], ORDER_FLOPS)
    square, ext = multiply_first(table, lefts, (next_chip, blocks, chip), window, slots)
    lefts, table = gather_rows(square, table, *HOW[1])
    part = multiply(SOON, table, lefts, ext, None, window, slots, jnp.float32)
    cube = multiply(LATE, table, lefts, ext, part, window, slots, jnp.bfloat16)
    return square, cube


def solution(mesh):
    placed = P("wide", "narrow", None, None)
    return jax.shard_map(
        per_device,
        mesh=mesh,
        in_specs=(placed, P(), P()),
        out_specs=(placed, placed),
        check_vma=False,
    )
```
